128 devices in a mesh: dp: 16 (over x, y_hi, core), seq: 8 (over y_lo, z).
Axes of the slice: x: 4, y: 4 (y_hi: 2, y_lo: 2; y = y_hi * 2 + y_lo), z: 4, core: 2. Of those that a mesh axis runs over, the one named last changes fastest.
Arguments:
- grad_out: bfloat16 [16384, 4096], P(('dp', 'seq')), may hold values from -6 to 6
- moe_input: bfloat16 [16384, 4096], P(('dp', 'seq')), may hold values from -900 to 900
- router_weight: bfloat16 [4096, 128], replicated, may hold values from -0.09375 to 0.09375
- routes: int32 [16384, 8], P(('dp', 'seq')), may hold values from 0 to 127, as said below
- gate_saved: bfloat16 [128, 128, 12, 768], P(('dp', 'seq')), may hold values from -8 to 8
- up_saved: bfloat16 [128, 128, 12, 768], P(('dp', 'seq')), may hold values from -6 to 6
- expert_gate: bfloat16 [128, 4096, 768], P(('dp', 'seq')), may hold values from -0.09375 to 0.09375
- expert_up: bfloat16 [128, 4096, 768], P(('dp', 'seq')), may hold values from -0.09375 to 0.09375
- expert_down: bfloat16 [128, 768, 4096], P(('dp', 'seq')), may hold values from -0.21875 to 0.21875
Outputs:
- input_grad: bfloat16 [16384, 4096], P(('dp', 'seq'))
- router_grad: float32 [128, 4096], P(('dp', 'seq'))
The draws below stay inside these ranges and needn't reach their ends.
Inputs may be any that keep to these rules, and one draw needn't show every extreme that they name: `routes`: among the picks of one block of 128 tokens, each expert is named at most 12 times, and some expert is named exactly 12 times in every block; the 8 picks of a token differ.
All inputs are finite; a program needn't handle non-finite values.
Results may differ from the reference program's by a relative error of at most 0.014.
Values may be sent and summed in bfloat16 or wider, within the bound.
A program may use at most 192 MiB of HBM per device.

```python
import jax
import jax.numpy as jnp
from jax import lax

D = 4096
TOP = 8
HW = 768
TOK_DEV = 128
EXPERT_TOTAL = 128
CAP = 12
TOKENS = 16384
DEVICES = 128


def block_arrangement(key, popular_boost):
    quiet_count = TOK_DEV // 16
    busy_count = TOK_DEV - quiet_count
    child_random_keys = jax.random.split(key, 3)
    block_jitter = jax.random.randint(child_random_keys[0], (EXPERT_TOTAL,), 0, 65536)
    block_rating = (popular_boost + block_jitter) * EXPERT_TOTAL + jnp.arange(EXPERT_TOTAL, dtype=jnp.int32)
    ranking_order = jnp.argsort(-block_rating).astype(jnp.int32)
    active = ranking_order[:EXPERT_TOTAL - TOP]
    spare_set = ranking_order[EXPERT_TOTAL - TOP:]
    quota_set = jax.random.randint(child_random_keys[1], (EXPERT_TOTAL - TOP,), max(1, CAP // 2), CAP + 1)
    quota_set = quota_set.at[0].set(CAP)
    pick_total = busy_count * TOP
    before = jnp.cumsum(quota_set) - quota_set
    first_fill = jnp.clip(pick_total - before, 0, quota_set)
    remain = pick_total - jnp.sum(first_fill)
    free_room = CAP - first_fill
    before_room = jnp.cumsum(free_room) - free_room
    counts = first_fill + jnp.clip(remain - before_room, 0, free_room)
    run_ends = jnp.cumsum(counts)
    places = jnp.arange(pick_total, dtype=jnp.int32)
    run_index = jnp.sum((places[:, None] >= run_ends[None, :]).astype(jnp.int32), axis=1)
    sequence = active[run_index].reshape(TOP, busy_count)
    rotation = (jnp.arange(TOP, dtype=jnp.int32)[None, :] + jnp.arange(busy_count, dtype=jnp.int32)[:, None]) % TOP
    busy_picks = jnp.take_along_axis(sequence.T, rotation, axis=1)
    quiet_turn = (jnp.arange(TOP, dtype=jnp.int32)[None, :] + jnp.arange(quiet_count, dtype=jnp.int32)[:, None]) % TOP
    quiet_picks = spare_set[quiet_turn]
    shuffled = jax.random.permutation(child_random_keys[2], TOK_DEV).astype(jnp.int32)
    block_routes = jnp.zeros((TOK_DEV, TOP), jnp.int32)
    block_routes = block_routes.at[shuffled[quiet_count:]].set(busy_picks)
    block_routes = block_routes.at[shuffled[:quiet_count]].set(quiet_picks)
    quiet_flag = jnp.zeros((TOK_DEV,), jnp.int32).at[shuffled[:quiet_count]].set(1)
    return (block_routes, quiet_flag)


def route_layout(key):
    pair_count = DEVICES // 2
    child_random_keys = jax.random.split(key, 4)
    expert_standing = jax.random.permutation(child_random_keys[0], EXPERT_TOTAL).astype(jnp.int32)
    popular_boost = expert_standing * 512 + jnp.where(expert_standing == EXPERT_TOTAL - 1, 131072, 0).astype(jnp.int32)
    couple_random_keys = jax.random.split(child_random_keys[1], pair_count)
    even_paths, even_silent_flags = jax.vmap(lambda child_random_key: block_arrangement(child_random_key, popular_boost))(couple_random_keys)
    lone_pair = jax.random.randint(child_random_keys[2], (), 0, pair_count)
    single_paths, single_silent_flags = block_arrangement(child_random_keys[3], popular_boost)
    pair_ids = jnp.arange(pair_count, dtype=jnp.int32)
    odd_routes = jnp.where((pair_ids == lone_pair)[:, None, None], single_paths[None], even_paths)
    routes_all = jnp.stack([even_paths, odd_routes], axis=1).reshape(TOKENS, TOP).astype(jnp.int32)
    return routes_all


def draw_routes(key, part):
    routes_all = route_layout(key)
    return routes_all


def draw_grad_out(key, part):
    key = jax.random.fold_in(key, 13)
    normal_base = jnp.clip(jax.random.normal(key, (TOKENS, D), jnp.float32), -6.0, 6.0)
    return normal_base.astype(jnp.bfloat16)


def draw_moe_input(key, part):
    key = jax.random.fold_in(key, 11)
    normal_base = jnp.clip(jax.random.normal(key, (TOKENS, D), jnp.float32), -6.0, 6.0)
    return normal_base.astype(jnp.bfloat16)


def draw_gate_saved(key, part):
    key = jax.random.fold_in(key, 17)
    values = jnp.clip(jax.random.normal(key, (EXPERT_TOTAL, DEVICES, CAP, HW), jnp.float32) * 1.5, -8.0, 8.0)
    return values.astype(jnp.bfloat16)


def draw_up_saved(key, part):
    key = jax.random.fold_in(key, 19)
    values = jnp.clip(jax.random.normal(key, (EXPERT_TOTAL, DEVICES, CAP, HW), jnp.float32), -6.0, 6.0)
    return values.astype(jnp.bfloat16)


def block_levels(key, extent, pieces, least, top_value):
    loudness = 1.0
    for dim, parts in pieces:
        heights = jax.random.uniform(jax.random.fold_in(jax.random.fold_in(key, 6), dim), (parts,), jnp.float32, least / len(pieces), top_value / len(pieces))
        loudness = loudness * jnp.repeat(jnp.exp(heights), extent[dim] // parts).reshape((-1,) + (1,) * (len(extent) - 1 - dim))
    return loudness


def scatter_about(rng, extent, scale, most, pieces=(), kind=jnp.bfloat16):
    drawn = scale * jax.random.normal(rng, extent, jnp.float32)
    if pieces:
        drawn = drawn * block_levels(rng, extent, pieces, -0.22, 0.18)
    return jnp.clip(drawn, -most, most).astype(kind)


def setup_inputs(seed: int = 0) -> dict:
    keys = jax.random.split(jax.random.key(seed), 10)
    return {
        "grad_out": draw_grad_out(jax.random.fold_in(keys[9], 71), 0),
        "moe_input": draw_moe_input(jax.random.fold_in(keys[9], 71), 0),
        "router_weight": scatter_about(keys[2], (D, EXPERT_TOTAL), D ** -0.5, 0.09375),
        "routes": draw_routes(jax.random.fold_in(keys[9], 71), 0),
        "gate_saved": draw_gate_saved(jax.random.fold_in(keys[9], 71), 0),
        "up_saved": draw_up_saved(jax.random.fold_in(keys[9], 71), 0),
        "expert_gate": scatter_about(keys[6], (EXPERT_TOTAL, D, HW), D ** -0.5, 0.09375, ((0, 128),)),
        "expert_up": scatter_about(keys[7], (EXPERT_TOTAL, D, HW), D ** -0.5, 0.09375, ((0, 128),)),
        "expert_down": scatter_about(keys[8], (EXPERT_TOTAL, HW, D), HW ** -0.5, 0.21875, ((0, 128),)),
    }


def expert_backward(rows, weights, gate_pre, up_pre, gate_weight, up_weight, down_weight):
    projected = lax.dot_general(rows, down_weight, (((1,), (1,)), ((), ())), preferred_element_type=jnp.float32)
    gate_value = gate_pre.astype(jnp.float32)
    up_value = up_pre.astype(jnp.float32)
    sigmoid_gate = jax.nn.sigmoid(gate_value)
    activated = gate_value * sigmoid_gate
    inner_sum = jnp.sum(projected * activated * up_value, axis=1).astype(jnp.bfloat16)
    scaled_grad = weights.astype(jnp.float32)[:, None] * projected
    gate_grad = (scaled_grad * up_value * sigmoid_gate * (1.0 + gate_value * (1.0 - sigmoid_gate))).astype(jnp.bfloat16)
    up_grad = (scaled_grad * activated).astype(jnp.bfloat16)
    summed = lax.dot_general(gate_grad, gate_weight, (((1,), (1,)), ((), ())), preferred_element_type=jnp.float32)
    summed = summed + lax.dot_general(up_grad, up_weight, (((1,), (1,)), ((), ())), preferred_element_type=jnp.float32)
    return summed.astype(jnp.bfloat16), inner_sum


def reference(grad_out, moe_input, router_weight, routes, gate_saved, up_saved, expert_gate, expert_up, expert_down):
    blocks = DEVICES
    per_block = TOK_DEV * TOP
    logits = jnp.dot(moe_input, router_weight, preferred_element_type=jnp.float32)
    expert_ids = jnp.arange(EXPERT_TOTAL, dtype=jnp.int32)
    picked = routes[:, :, None] == expert_ids[None, None, :]
    chosen = jnp.sum(jnp.where(picked, logits[:, None, :], jnp.float32(0.0)), axis=-1)
    highest = jnp.max(chosen, axis=1, keepdims=True)
    raised = jnp.exp(chosen - highest)
    combine = raised / jnp.sum(raised, axis=1, keepdims=True)
    combine_sent = combine.astype(jnp.bfloat16)
    targets = routes.reshape(blocks, per_block)
    onehot = (targets[:, :, None] == expert_ids[None, None, :]).astype(jnp.int32)
    ranking = jnp.cumsum(onehot, axis=1) - 1
    slot_index = jnp.sum(ranking * onehot, axis=2).astype(jnp.int32)
    position = (targets * CAP + slot_index).astype(jnp.int32)
    block_ids = jnp.arange(blocks, dtype=jnp.int32)[:, None]
    token_of = jnp.broadcast_to(jnp.arange(per_block, dtype=jnp.int32) // TOP, (blocks, per_block))
    lookup = jnp.full((blocks, EXPERT_TOTAL * CAP), TOK_DEV, jnp.int32).at[block_ids, position].set(token_of)
    weight_lookup = jnp.zeros((blocks, EXPERT_TOTAL * CAP), jnp.bfloat16).at[block_ids, position].set(combine_sent.reshape(blocks, per_block))
    padded = jnp.concatenate([grad_out.reshape(blocks, TOK_DEV, D), jnp.zeros((blocks, 1, D), jnp.bfloat16)], axis=1)

    def one_expert(running, expert):
        start = (expert * CAP).astype(jnp.int32)
        index = lax.dynamic_slice_in_dim(lookup, start, CAP, 1)
        rows = padded[block_ids, index]
        weights = lax.dynamic_slice_in_dim(weight_lookup, start, CAP, 1)
        summed, inner_sum = expert_backward(rows.reshape(blocks * CAP, D), weights.reshape(blocks * CAP),
                                            gate_saved[expert].reshape(blocks * CAP, HW),
                                            up_saved[expert].reshape(blocks * CAP, HW),
                                            expert_gate[expert], expert_up[expert], expert_down[expert])
        running = running.at[block_ids, index].add(summed.reshape(blocks, CAP, D).astype(jnp.float32))
        return running, inner_sum.reshape(blocks, CAP)

    running, inner_all = lax.scan(one_expert, jnp.zeros((blocks, TOK_DEV + 1, D), jnp.float32), expert_ids)
    pick_score = inner_all[targets, block_ids, slot_index].reshape(TOKENS, TOP).astype(jnp.float32)
    chosen_grad = combine * (pick_score - jnp.sum(combine * pick_score, axis=1, keepdims=True))
    logit_grad = jnp.sum(jnp.where(picked, chosen_grad[:, :, None], jnp.float32(0.0)), axis=1).astype(jnp.bfloat16)
    routed = lax.dot_general(logit_grad, router_weight, (((1,), (1,)), ((), ())), preferred_element_type=jnp.float32)
    moe_part = running[:, :TOK_DEV, :].reshape(TOKENS, D)
    input_grad = (moe_part + routed).astype(jnp.bfloat16)
    router_grad = lax.dot_general(logit_grad, moe_input, (((0,), (0,)), ((), ())), preferred_element_type=jnp.float32)
    return input_grad, router_grad
```

```python
import jax
import jax.numpy as jnp
from jax import lax
from jax.experimental import pallas as pl
from jax.experimental.pallas import tpu as pltpu
from jax.sharding import PartitionSpec as P

MESH = pl.DeviceIdType.MESH
F32, BF16 = jnp.float32, jnp.bfloat16
COL = 1024
LAST = 3 * COL
HID = 768
SLOTS = 12


def nt(a, b):
    return lax.dot_general(a, b, (((1,), (1,)), ((), ())), preferred_element_type=F32)


def nn(a, b):
    return lax.dot_general(a, b, (((1,), (0,)), ((), ())), preferred_element_type=F32)


def iota(shape, dim):
    return lax.broadcasted_iota(jnp.int32, shape, dim)


def onehot(cond):
    return jnp.where(cond, 1.0, 0.0).astype(BF16)


def device(x, y, z, c):
    return (x * 4 + (y // 2) * 2 + c, (y % 2) * 4 + z)


def expert_id(x, y, z, c):
    return x * 32 + (y // 2) * 16 + c * 8 + (y % 2) * 4 + z


def plane_member(part, ahead, b, here, c):
    x, y, z = here
    return (
        (x, (y + ahead) % 4, b, c),
        (b, y, (z + ahead) % 4, c),
        ((x + ahead) % 4, b, z, c),
    )[part]


def line_member(part, position, here, c):
    x, y, z = here
    return ((position, y, z, c), (x, position, z, c), (x, y, position, c))[part]


def kernel(
    x_ref, h_ref, rw_ref, routes_ref, gs_hbm, us_hbm, wg_hbm, wu_hbm, wd_hbm,
    out_ref, router_ref, back_hbm,
    gathered, meta, staged, landed, wd, wg, wu, gs_buf, us_buf,
    expand, combine_ref, slots_ref, score_rows, score_send, score_plane, score_line,
    score_all, terms_in, rows_out, rows_in,
    w_sem, gs_sem, ax_send, ax_recv, am_send, am_recv, own_sem,
    d_send, d_recv, r_send, r_recv, sp_send, sp_recv, sl_send, sl_recv,
    t_send, t_recv, q_send, q_recv, load_sem, p_send, p_recv,
):
    dp, seq = lax.axis_index("dp"), lax.axis_index("seq")
    x, c, z = dp // 4, dp % 2, seq % 4
    yh, yl = (dp // 2) % 2, seq // 4
    y = yh * 2 + yl
    here = (x, y, z)
    second = (z, x, y)
    sign = 1 - 2 * c
    my_plane = (dp % 4) * 8 + seq

    def weight_copies():
        copies = []
        for p in range(4):
            columns = pl.ds(p * COL, COL)
            copies.append(pltpu.make_async_copy(wd_hbm.at[:, columns], wd.at[p], w_sem.at[p]))
        copies.append(pltpu.make_async_copy(wg_hbm, wg, w_sem.at[4]))
        copies.append(pltpu.make_async_copy(wu_hbm, wu, w_sem.at[5]))
        return copies

    for copy in weight_copies():
        copy.start()

    barrier = pltpu.get_barrier_semaphore()

    def greet(target):
        pl.semaphore_signal(barrier, inc=1, device_id=device(*target), device_id_type=MESH)

    def greet_x(k, carry):
        greet((x, (y + k // 8) % 4, (z + (k // 2) % 4) % 4, (c + k % 2) % 2))
        return carry

    def greet_y(k, carry):
        greet(((x + 1 + k // 8) % 4, y, (z + (k // 2) % 4) % 4, (c + k % 2) % 2))
        return carry

    def greet_z(k, carry):
        greet(((x + 1 + k // 6) % 4, (y + 1 + (k // 2) % 3) % 4, z, (c + k % 2) % 2))
        return carry

    lax.fori_loop(1, 32, greet_x, 0)
    lax.fori_loop(0, 24, greet_y, 0)
    lax.fori_loop(0, 18, greet_z, 0)

    square = (128, 128)
    picked_t = jnp.zeros(square, F32)
    for k in range(8):
        picked_t = picked_t + jnp.where(routes_ref[k : k + 1, :] == iota(square, 0), 1.0, 0.0)
    picked_t = picked_t.astype(BF16)
    picked = nt(onehot(iota(square, 0) == iota(square, 1)), picked_t) > 0.5
    earlier = nt(onehot(iota(square, 1) < iota(square, 0)), picked_t)
    slots = jnp.where(picked, earlier, -1.0)
    slots_ref[...] = slots

    pl.semaphore_wait(barrier, 73)

    def token_copies(part, step):
        position = (here[part] + step) % 4
        to = device(*line_member(part, position, here, c))
        return [
            pltpu.make_async_remote_copy(
                src_ref=x_ref.at[:, pl.ds(first, COL)],
                dst_ref=gathered.at[part, here[part], pl.ds(128 * n, 128)],
                send_sem=ax_send.at[part, step, n],
                recv_sem=ax_recv.at[part, here[part], n],
                device_id=to,
                device_id_type=MESH,
            )
            for n, first in enumerate((part * COL, LAST))
        ]

    for step in (1, 3, 2):
        for part in range(3):
            for copy in token_copies(part, step):
                copy.start()

    logits = nn(h_ref[...], rw_ref[...])
    highest = jnp.max(jnp.where(picked, logits, -jnp.inf), axis=1, keepdims=True)
    raised = jnp.where(picked, jnp.exp(jnp.where(picked, logits, highest) - highest), 0.0)
    combine = raised / jnp.sum(raised, axis=1, keepdims=True)
    combine_ref[...] = combine
    for part in range(3):
        meta[part, here[part], 0:128, :] = slots.astype(BF16)
        meta[part, here[part], 128:256, :] = combine.astype(BF16)

    def meta_copy(part, step):
        position = (here[part] + step) % 4
        return pltpu.make_async_remote_copy(
            src_ref=meta.at[part, here[part]],
            dst_ref=meta.at[part, here[part]],
            send_sem=am_send.at[part, step],
            recv_sem=am_recv.at[part, here[part]],
            device_id=device(*line_member(part, position, here, c)),
            device_id_type=MESH,
        )

    for step in (1, 3, 2):
        for part in range(3):
            meta_copy(part, step).start()

    for part in range(3):
        gathered[part, here[part], 0:128, :] = x_ref[:, part * COL : (part + 1) * COL]
        gathered[part, here[part], 128:256, :] = x_ref[:, LAST:]

    row, lane = iota((512, 128), 0), iota((512, 128), 1)
    ahead = sign * (row // 128) + 4
    core = (c + (row // 64) % 2) % 2
    b = (row // 16) % 4
    for part in range(3):
        owner = expert_id(*plane_member(part, ahead, b, here, core))
        expand[part] = onehot(owner == lane)

    def message(buffer, part, a, dc, b):
        if part == 1:
            return buffer.at[1, a, :, dc, :, b]
        return buffer.at[part, a, dc, b // 2, b % 2]

    def dispatch_copy(part, k):
        a, dc, b = k // 8, (k // 4) % 2, (second[part] + k % 4) % 4
        to = plane_member(part, sign * a + 4, b, here, (c + dc) % 2)
        landing = (
            landed.at[0, :, yh, c, yl, z],
            landed.at[1, x, :, c, :, z],
            landed.at[2, x, yh, c, yl],
        )[part]
        return pltpu.make_async_remote_copy(
            src_ref=message(staged, part, a, dc, b),
            dst_ref=landing,
            send_sem=d_send.at[part, k],
            recv_sem=d_recv.at[part, a * 8 + dc * 4 + second[part]],
            device_id=device(*to),
            device_id_type=MESH,
        )

    def own_copy(part):
        landing = (
            landed.at[0, :, yh, c, yl, z],
            landed.at[1, x, :, c, :, z],
            landed.at[2, x, yh, c, yl],
        )[part]
        return pltpu.make_async_copy(
            message(staged, part, 0, 0, second[part]), landing, own_sem.at[part]
        )

    slot_of_row = iota((512, 128), 0) % 16

    def wait_line(part):
        for step in (1, 2, 3):
            position = (here[part] + step) % 4
            for n in range(2):
                pltpu.make_async_remote_copy(
                    src_ref=gathered.at[part, position, pl.ds(128 * n, 128)],
                    dst_ref=gathered.at[part, position, pl.ds(128 * n, 128)],
                    send_sem=ax_send.at[part, step, n],
                    recv_sem=ax_recv.at[part, position, n],
                    device_id=device(*line_member(part, position, here, c)),
                    device_id_type=MESH,
                ).wait_recv()
            pltpu.make_async_remote_copy(
                src_ref=meta.at[part, position],
                dst_ref=meta.at[part, position],
                send_sem=am_send.at[part, step],
                recv_sem=am_recv.at[part, position],
                device_id=device(*line_member(part, position, here, c)),
                device_id_type=MESH,
            ).wait_recv()

    def extra_slot(part):
        return jnp.where(slot_of_row >= SLOTS, slot_of_row - SLOTS + 4 * part, -9).astype(F32)

    for part in range(3):
        wait_line(part)

    for half in range(2):
        for part in range(3):

            def select(j, carry, part=part, half=half):
                rows = slice(256 * half, 256 * half + 256)
                spread = nt(expand[part, rows, :], meta[part, j, 0:128, :])
                main = onehot(spread == slot_of_row[rows].astype(F32))
                extra = onehot(spread == extra_slot(part)[rows])
                chosen = jnp.concatenate([main, extra], axis=1)
                made = nn(chosen, gathered[part, j]).astype(BF16)
                if part == 1:
                    staged[1, 2 * half : 2 * half + 2, j // 2, :, j % 2] = made.reshape(
                        2, 2, 4, 16, COL
                    )
                else:
                    staged[part, 2 * half : 2 * half + 2, :, :, :, j] = made.reshape(
                        2, 2, 2, 2, 16, COL
                    )
                return carry

            lax.fori_loop(0, 4, select, 0)

        def send(k, carry):
            for part in range(3):
                dispatch_copy(part, k).start()
            return carry

        lax.fori_loop(1 if half == 0 else 16, 16 if half == 0 else 32, send, 0)
        if half == 0:
            for part in range(3):
                own_copy(part).start()

    def saved_copies(g, buffer):
        rows = pl.ds(pl.multiple_of(g * 16, 16), 16)
        return (
            pltpu.make_async_copy(gs_hbm.at[:, rows, :], gs_buf.at[buffer], gs_sem.at[0, buffer]),
            pltpu.make_async_copy(us_hbm.at[:, rows, :], us_buf.at[buffer], gs_sem.at[1, buffer]),
        )

    for copy in saved_copies(0, 0):
        copy.start()
    for copy in weight_copies():
        copy.wait()
    for part in range(3):
        own_copy(part).wait()

    def settle_dispatch(k, carry):
        for part in range(3):
            copy = dispatch_copy(part, k)
            copy.wait_send()
            a, dc, b = k // 8, (k // 4) % 2, (second[part] + k % 4) % 4
            pltpu.make_async_remote_copy(
                src_ref=message(staged, part, a, dc, b),
                dst_ref=message(landed, part, a, dc, b),
                send_sem=d_send.at[part, k],
                recv_sem=d_recv.at[part, a * 8 + dc * 4 + b],
                device_id=device(x, y, z, 1 - c),
                device_id_type=MESH,
            ).wait_recv()
        return carry

    lax.fori_loop(1, 32, settle_dispatch, 0)

    big = (256, 256)
    to_row, from_row = iota(big, 0), iota(big, 1)
    same_source = to_row // 16 == from_row // 16
    moves = [
        onehot(
            same_source
            & (from_row % 16 >= SLOTS)
            & (to_row % 16 == from_row % 16 - SLOTS + 4 * part)
        )
        for part in range(3)
    ]
    take = (256, 16 * SLOTS)
    by_source = onehot(
        (iota(take, 0) // 16 == iota(take, 1) % 16) & (iota(take, 0) % 16 == iota(take, 1) // 16)
    )
    diagonal = iota((128, 128), 0) == iota((128, 128), 1)

    def expert_group(g, carry):
        gx, gy = g // 2, g % 2
        buffer = g % 2

        @pl.when(g < 7)
        def _():
            for copy in saved_copies(g + 1, (g + 1) % 2):
                copy.start()

        for copy in saved_copies(g, buffer):
            copy.wait()
        rows = [landed[part, gx, gy].reshape(256, COL) for part in range(3)]
        last = (nn(moves[0], rows[0]) + nn(moves[1], rows[1]) + nn(moves[2], rows[2])).astype(BF16)
        projected = (
            nt(rows[0], wd[0]) + nt(rows[1], wd[1]) + nt(rows[2], wd[2]) + nt(last, wd[3])
        )
        gate = nn(by_source, gs_buf[buffer].reshape(16 * SLOTS, HID))
        up = nn(by_source, us_buf[buffer].reshape(16 * SLOTS, HID))
        sigmoid = jax.nn.sigmoid(gate)
        activated = gate * sigmoid
        up_grad = projected * activated
        inner = jnp.sum(up_grad * up, axis=1, keepdims=True)
        gate_grad = projected * up * sigmoid * (1.0 + gate * (1.0 - sigmoid))
        shape = (2, 2, 4, 16, HID)
        staged[0, gx, gy, :, :, :, :, 0:HID] = gate_grad.astype(BF16).reshape(shape)
        staged[1, gx, gy, :, :, :, :, 0:HID] = up_grad.astype(BF16).reshape(shape)
        for n in range(2):
            column = inner[128 * n : 128 * n + 128]
            line = jnp.sum(jnp.where(diagonal, column, 0.0), axis=0, keepdims=True)
            score_rows[pl.ds(g * 2 + n, 1), :] = line
        return carry

    lax.fori_loop(0, 8, expert_group, 0)

    score_send[...] = score_rows[...].astype(BF16)

    def plane_peer(k):
        to = plane_member(0, k // 8, (z + k % 4) % 4, here, (c + (k // 4) % 2) % 2)
        ids = device(*to)
        return ids, (ids[0] % 4) * 8 + ids[1]

    def score_copy(k):
        ids, _ = plane_peer(k)
        return pltpu.make_async_remote_copy(
            src_ref=score_send,
            dst_ref=score_plane.at[my_plane],
            send_sem=sp_send.at[k],
            recv_sem=sp_recv.at[my_plane],
            device_id=ids,
            device_id_type=MESH,
        )

    def start_score(k, carry):
        score_copy(k).start()
        return carry

    lax.fori_loop(1, 32, start_score, 0)
    score_plane[my_plane] = score_send[...]

    def return_copy(part, k):
        a, dc, b = k // 8, (k // 4) % 2, (second[part] + k % 4) % 4
        relay_core = (c + dc) % 2
        to = plane_member(part, 4 - (1 - 2 * relay_core) * a, b, here, relay_core)
        return pltpu.make_async_remote_copy(
            src_ref=message(landed, part, a, dc, b),
            dst_ref=message(back_hbm, part, a, dc, second[part]),
            send_sem=r_send.at[part, k],
            recv_sem=r_recv.at[part, a * 8 + dc * 4 + second[part]],
            device_id=device(*to),
            device_id_type=MESH,
        )

    def own_return(part):
        b = second[part]
        return pltpu.make_async_copy(
            message(landed, part, 0, 0, b), message(back_hbm, part, 0, 0, b), own_sem.at[part]
        )

    row_slot = iota((256, COL), 0) % 16

    def expert_unit(u, carry):
        a, dc = u // 2, u % 2
        relay_core = (c + dc) % 2
        ahead = 4 - (1 - 2 * relay_core) * a
        for part in range(3):
            place = (here[(part + 1) % 3] if part != 1 else z) + ahead
            if part == 0:
                ry = (y + ahead) % 4
                pair = [staged[n, :, ry // 2, relay_core, ry % 2, :, :, 0:HID] for n in range(2)]
            elif part == 1:
                rz = (z + ahead) % 4
                pair = [staged[n, :, :, relay_core, :, rz, :, 0:HID] for n in range(2)]
            else:
                rx = (x + ahead) % 4
                pair = [staged[n, rx, :, relay_core, :, :, :, 0:HID] for n in range(2)]
            gate_grad, up_grad = (v.reshape(256, HID) for v in pair)
            main = nt(gate_grad, wg[part * COL : (part + 1) * COL, :]) + nt(
                up_grad, wu[part * COL : (part + 1) * COL, :]
            )
            last = nt(gate_grad, wg[LAST:, :]) + nt(up_grad, wu[LAST:, :])
            made = jnp.where(
                row_slot < SLOTS, main, pltpu.roll(last, SLOTS - 4 * part, axis=0)
            ).astype(BF16)
            if part == 0:
                made = made.reshape(4, 4, 16, COL)
                for b in range(4):
                    landed[0, a, dc, b // 2, b % 2] = made[:, b]
            elif part == 1:
                made = made.reshape(4, 2, 2, 16, COL)
                for b in range(4):
                    landed[1, a, :, dc, :, b] = made[b]
            else:
                landed[2, a, dc] = made.reshape(2, 2, 4, 16, COL)

        def send(k, carry):
            for part in range(3):
                return_copy(part, k).start()
            return carry

        @pl.when(u == 0)
        def _():
            for part in range(3):
                own_return(part).start()

        lax.fori_loop(jnp.where(u == 0, 1, 4 * u), 4 * u + 4, send, 0)
        return carry

    lax.fori_loop(0, 8, expert_unit, 0)

    def settle_score(k, carry):
        score_copy(k).wait_send()
        ids, index = plane_peer(k)
        pltpu.make_async_remote_copy(
            src_ref=score_send,
            dst_ref=score_plane.at[index],
            send_sem=sp_send.at[k],
            recv_sem=sp_recv.at[index],
            device_id=ids,
            device_id_type=MESH,
        ).wait_recv()
        return carry

    lax.fori_loop(1, 32, settle_score, 0)
    plane_scores = score_plane[...].reshape(512, 128)
    for position in range(4):
        wanted = position * 4 + yh * 2 + c
        pickup = onehot(iota((32, 512), 1) == iota((32, 512), 0) * 16 + wanted)
        score_line[position] = nn(pickup, plane_scores).astype(BF16)

    def line_ids(step):
        return device((x + step) % 4, y, z, c)

    def line_score_copy(step):
        return pltpu.make_async_remote_copy(
            src_ref=score_line.at[(x + step) % 4],
            dst_ref=score_all.at[x],
            send_sem=sl_send.at[step],
            recv_sem=sl_recv.at[x],
            device_id=line_ids(step),
            device_id_type=MESH,
        )

    for step in (1, 2, 3):
        line_score_copy(step).start()
    score_all[x] = score_line[x]
    for step in (1, 2, 3):
        position = (x + step) % 4
        line_score_copy(step).wait_send()
        pltpu.make_async_remote_copy(
            src_ref=score_line.at[position],
            dst_ref=score_all.at[position],
            send_sem=sl_send.at[step],
            recv_sem=sl_recv.at[position],
            device_id=line_ids(step),
            device_id_type=MESH,
        ).wait_recv()

    mine = onehot(iota((16, 128), 1) == iota((16, 128), 0) + seq * 16)
    by_slot = nt(mine, score_all[...].reshape(128, 128))
    slots = slots_ref[...]
    combine = combine_ref[...]
    score = jnp.zeros(square, F32)
    for n in range(SLOTS):
        score = score + jnp.where(slots == float(n), by_slot[n : n + 1, :], 0.0)
    weighted = combine * score
    logit_grad = (weighted - combine * jnp.sum(weighted, axis=1, keepdims=True)).astype(BF16)
    logit_grad_t = nt(onehot(iota(square, 0) == iota(square, 1)), logit_grad).astype(BF16)
    for n in range(4):
        terms = nn(logit_grad_t, h_ref[:, n * COL : (n + 1) * COL]).astype(BF16)
        for m in range(8):
            staged[2, m // 2, n // 2, n % 2, m % 2, 0] = terms[16 * m : 16 * m + 16]

    def terms_copy(step):
        return pltpu.make_async_remote_copy(
            src_ref=staged.at[2, (x + step) % 4, :, :, :, 0],
            dst_ref=terms_in.at[x],
            send_sem=t_send.at[step],
            recv_sem=t_recv.at[x],
            device_id=line_ids(step),
            device_id_type=MESH,
        )

    for step in (1, 2, 3):
        terms_copy(step).start()
    total = staged[2, x, :, :, :, 0].astype(F32)
    for step in (1, 2, 3):
        position = (x + step) % 4
        terms_copy(step).wait_send()
        pltpu.make_async_remote_copy(
            src_ref=staged.at[2, position, :, :, :, 0],
            dst_ref=terms_in.at[position],
            send_sem=t_send.at[step],
            recv_sem=t_recv.at[position],
            device_id=line_ids(step),
            device_id_type=MESH,
        ).wait_recv()
        total = total + terms_in[position].astype(F32)
    for n in range(8):
        for m in range(2):
            block = total[n // 4, (n // 2) % 2, m]
            rows_out[16 * m : 16 * m + 16, n, :] = block[:, 512 * (n % 2) : 512 * (n % 2) + 512]

    def rows_copy(k):
        ids, index = plane_peer(k)
        return pltpu.make_async_remote_copy(
            src_ref=rows_out.at[index],
            dst_ref=rows_in.at[my_plane],
            send_sem=q_send.at[k],
            recv_sem=q_recv.at[my_plane],
            device_id=ids,
            device_id_type=MESH,
        )

    def start_rows(k, carry):
        rows_copy(k).start()
        return carry

    lax.fori_loop(1, 32, start_rows, 0)
    rows_in[my_plane] = rows_out[my_plane]

    for part in range(3):
        own_return(part).wait()

    def settle_return(k, carry):
        for part in range(3):
            return_copy(part, k).wait_send()
            a, dc, b = k // 8, (k // 4) % 2, (second[part] + k % 4) % 4
            pltpu.make_async_remote_copy(
                src_ref=message(landed, part, a, dc, b),
                dst_ref=message(back_hbm, part, a, dc, b),
                send_sem=r_send.at[part, k],
                recv_sem=r_recv.at[part, a * 8 + dc * 4 + b],
                device_id=device(x, y, z, 1 - c),
                device_id_type=MESH,
            ).wait_recv()
        return carry

    lax.fori_loop(1, 32, settle_return, 0)

    def load_copy(part):
        return pltpu.make_async_copy(back_hbm.at[part], staged.at[part], load_sem.at[part])

    for part in range(3):
        load_copy(part).start()

    def line_slot(part, position):
        n = part * 4 + position
        return wd.at[n // 3, pl.ds(pl.multiple_of((n % 3) * 256, 256), 256)]

    def part_copy(part, step):
        position = (here[part] + step) % 4
        return pltpu.make_async_remote_copy(
            src_ref=gathered.at[part, position],
            dst_ref=line_slot(part, here[part]),
            send_sem=p_send.at[part, step],
            recv_sem=p_recv.at[part, here[part]],
            device_id=device(*line_member(part, position, here, c)),
            device_id_type=MESH,
        )

    for part in range(3):
        load_copy(part).wait()
        lane_slot = iota((128, 512), 1) % 16
        lane_extra = jnp.where(lane_slot >= SLOTS, lane_slot - SLOTS + 4 * part, -9).astype(F32)

        def gather_back(step, carry, part=part, lane_slot=lane_slot, lane_extra=lane_extra):
            j = (here[part] + step) % 4
            spread = nt(meta[part, j, 0:128, :], expand[part])
            weight = nt(meta[part, j, 128:256, :], expand[part])
            main = jnp.where(spread == lane_slot.astype(F32), weight, 0.0).astype(BF16)
            extra = jnp.where(spread == lane_extra, weight, 0.0).astype(BF16)
            if part == 1:
                rows = staged[1, :, j // 2, :, j % 2]
            else:
                rows = staged[part, :, :, :, :, j]
            rows = rows.reshape(512, COL)
            gathered[part, j, 0:128, :] = nn(main, rows).astype(BF16)
            gathered[part, j, 128:256, :] = nn(extra, rows).astype(BF16)

            @pl.when(step > 0)
            def _():
                part_copy(part, step).start()

            return carry

        lax.fori_loop(0, 4, gather_back, 0)

    routed = [nt(logit_grad, rw_ref[n * COL : (n + 1) * COL, :]) for n in range(4)]
    tail = routed[3]
    for part in range(3):
        head = routed[part] + gathered[part, here[part], 0:128, :].astype(F32)
        tail = tail + gathered[part, here[part], 128:256, :].astype(F32)
        for step in (1, 2, 3):
            position = (here[part] + step) % 4
            part_copy(part, step).wait_send()
            arrived = line_slot(part, position)
            pltpu.make_async_remote_copy(
                src_ref=gathered.at[part, position],
                dst_ref=arrived,
                send_sem=p_send.at[part, step],
                recv_sem=p_recv.at[part, position],
                device_id=device(*line_member(part, position, here, c)),
                device_id_type=MESH,
            ).wait_recv()
            head = head + arrived[0:128, :].astype(F32)
            tail = tail + arrived[128:256, :].astype(F32)
        out_ref[:, part * COL : (part + 1) * COL] = head.astype(BF16)
    out_ref[:, LAST:] = tail.astype(BF16)

    def settle_rows(k, carry):
        rows_copy(k).wait_send()
        ids, index = plane_peer(k)
        pltpu.make_async_remote_copy(
            src_ref=rows_out.at[index],
            dst_ref=rows_in.at[index],
            send_sem=q_send.at[k],
            recv_sem=q_recv.at[index],
            device_id=ids,
            device_id_type=MESH,
        ).wait_recv()
        return carry

    lax.fori_loop(1, 32, settle_rows, 0)
    router_ref[...] = jnp.sum(rows_in[...], axis=0)

    for part in range(3):
        for step in (1, 2, 3):
            for copy in token_copies(part, step):
                copy.wait_send()
            meta_copy(part, step).wait_send()


def shards(
    grad_out,
    moe_input,
    router_weight,
    routes,
    gate_saved,
    up_saved,
    expert_gate,
    expert_up,
    expert_down,
):
    dma = pltpu.SemaphoreType.DMA
    whole = pl.BlockSpec(memory_space=pltpu.VMEM)
    away = pl.BlockSpec(memory_space=pl.ANY)
    blocks = (3, 4, 2, 2, 2, 4, 16, COL)
    input_grad, router_grad, _ = pl.pallas_call(
        kernel,
        out_shape=(
            jax.ShapeDtypeStruct((128, 4096), BF16),
            jax.ShapeDtypeStruct((8, 512), F32),
            jax.ShapeDtypeStruct(blocks, BF16),
        ),
        in_specs=[whole] * 4 + [away] * 5,
        out_specs=(whole, whole, away),
        scratch_shapes=[
            pltpu.VMEM((3, 4, 256, COL), BF16),
            pltpu.VMEM((3, 4, 256, 128), BF16),
            pltpu.VMEM(blocks, BF16),
            pltpu.VMEM(blocks, BF16),
            pltpu.VMEM((4, HID, COL), BF16),
            pltpu.VMEM((4096, HID), BF16),
            pltpu.VMEM((4096, HID), BF16),
            pltpu.VMEM((2, SLOTS, 16, HID), BF16),
            pltpu.VMEM((2, SLOTS, 16, HID), BF16),
            pltpu.VMEM((3, 512, 128), BF16),
            pltpu.VMEM((128, 128), F32),
            pltpu.VMEM((128, 128), F32),
            pltpu.VMEM((16, 128), F32),
            pltpu.VMEM((16, 128), BF16),
            pltpu.VMEM((32, 16, 128), BF16),
            pltpu.VMEM((4, 32, 128), BF16),
            pltpu.VMEM((4, 32, 128), BF16),
            pltpu.VMEM((4, 2, 2, 2, 16, COL), BF16),
            pltpu.VMEM((32, 8, 512), F32),
            pltpu.VMEM((32, 8, 512), F32),
            dma((6,)),
            dma((2, 2)),
            dma((3, 4, 2)),
            dma((3, 4, 2)),
            dma((3, 4)),
            dma((3, 4)),
            dma((3,)),
            dma((3, 32)),
            dma((3, 32)),
            dma((3, 32)),
            dma((3, 32)),
            dma((32,)),
            dma((32,)),
            dma((4,)),
            dma((4,)),
            dma((4,)),
            dma((4,)),
            dma((32,)),
            dma((32,)),
            dma((3,)),
            dma((3, 4)),
            dma((3, 4)),
        ],
        compiler_params=pltpu.CompilerParams(
            collective_id=0, has_side_effects=True, vmem_limit_bytes=62 << 20
        ),
        cost_estimate=pl.CostEstimate(
            flops=80_000_000_000, bytes_accessed=60 << 20, transcendentals=2 << 20
        ),
    )(
        grad_out,
        moe_input,
        router_weight,
        routes.T,
        jnp.transpose(gate_saved[0], (1, 0, 2)),
        jnp.transpose(up_saved[0], (1, 0, 2)),
        expert_gate[0],
        expert_up[0],
        expert_down[0],
    )
    return (input_grad, router_grad.reshape(1, 4096))


def solution(mesh):
    placed = (
        P(("dp", "seq"), None),
        P(("dp", "seq"), None),
        P(),
        P(("dp", "seq"), None),
        P(("dp", "seq"), None, None, None),
        P(("dp", "seq"), None, None, None),
        P(("dp", "seq"), None, None),
        P(("dp", "seq"), None, None),
        P(("dp", "seq"), None, None),
    )
    return jax.shard_map(
        shards,
        mesh=mesh,
        in_specs=placed,
        out_specs=(P(("dp", "seq"), None), P(("dp", "seq"), None)),
        check_vma=False,
    )
```

```python
import jax
import jax.numpy as jnp
from jax import lax
from jax.experimental import pallas as pl
from jax.experimental.pallas import tpu as pltpu
from jax.sharding import PartitionSpec as P

MESH = pl.DeviceIdType.MESH
F32, BF16 = jnp.float32, jnp.bfloat16
COL = 1024
LAST = 3 * COL
HID = 768
SLOTS = 12


def nt(a, b):
    return lax.dot_general(a, b, (((1,), (1,)), ((), ())), preferred_element_type=F32)


def nn(a, b):
    return lax.dot_general(a, b, (((1,), (0,)), ((), ())), preferred_element_type=F32)


def iota(shape, dim):
    return lax.broadcasted_iota(jnp.int32, shape, dim)


def onehot(cond):
    return jnp.where(cond, 1.0, 0.0).astype(BF16)


def device(x, y, z, c):
    return (x * 4 + (y // 2) * 2 + c, (y % 2) * 4 + z)


def expert_id(x, y, z, c):
    return x * 32 + (y // 2) * 16 + c * 8 + (y % 2) * 4 + z


def plane_member(part, ahead, b, here, c):
    x, y, z = here
    return (
        (x, (y + ahead) % 4, b, c),
        (b, y, (z + ahead) % 4, c),
        ((x + ahead) % 4, b, z, c),
    )[part]


def line_member(part, position, here, c):
    x, y, z = here
    return ((position, y, z, c), (x, position, z, c), (x, y, position, c))[part]


def kernel(
    x_ref, h_ref, rw_ref, routes_ref, gs_hbm, us_hbm, wg_hbm, wu_hbm, wd_hbm,
    out_ref, router_ref, back_hbm,
    gathered, meta, staged, landed, wd, wg, wu, gs_buf, us_buf,
    expand, combine_ref, slots_ref, score_rows, score_send, score_plane, score_line,
    score_all, terms_in, rows_out, rows_in,
    w_sem, gs_sem, ax_send, ax_recv, am_send, am_recv, own_sem,
    d_send, d_recv, r_send, r_recv, sp_send, sp_recv, sl_send, sl_recv,
    t_send, t_recv, q_send, q_recv, load_sem, p_send, p_recv,
):
    dp, seq = lax.axis_index("dp"), lax.axis_index("seq")
    x, c, z = dp // 4, dp % 2, seq % 4
    yh, yl = (dp // 2) % 2, seq // 4
    y = yh * 2 + yl
    here = (x, y, z)
    second = (z, x, y)
    sign = 1 - 2 * c
    my_plane = (dp % 4) * 8 + seq

    def weight_copies():
        copies = []
        for p in range(4):
            columns = pl.ds(p * COL, COL)
            copies.append(pltpu.make_async_copy(wd_hbm.at[:, columns], wd.at[p], w_sem.at[p]))
        copies.append(pltpu.make_async_copy(wg_hbm, wg, w_sem.at[4]))
        copies.append(pltpu.make_async_copy(wu_hbm, wu, w_sem.at[5]))
        return copies

    for copy in weight_copies():
        copy.start()

    barrier = pltpu.get_barrier_semaphore()

    def greet(target):
        pl.semaphore_signal(barrier, inc=1, device_id=device(*target), device_id_type=MESH)

    def greet_x(k, carry):
        greet((x, (y + k // 8) % 4, (z + (k // 2) % 4) % 4, (c + k % 2) % 2))
        return carry

    def greet_y(k, carry):
        greet(((x + 1 + k // 8) % 4, y, (z + (k // 2) % 4) % 4, (c + k % 2) % 2))
        return carry

    def greet_z(k, carry):
        greet(((x + 1 + k // 6) % 4, (y + 1 + (k // 2) % 3) % 4, z, (c + k % 2) % 2))
        return carry

    lax.fori_loop(1, 32, greet_x, 0)
    lax.fori_loop(0, 24, greet_y, 0)
    lax.fori_loop(0, 18, greet_z, 0)

    square = (128, 128)
    picked_t = jnp.zeros(square, F32)
    for k in range(8):
        picked_t = picked_t + jnp.where(routes_ref[k : k + 1, :] == iota(square, 0), 1.0, 0.0)
    picked_t = picked_t.astype(BF16)
    picked = nt(onehot(iota(square, 0) == iota(square, 1)), picked_t) > 0.5
    earlier = nt(onehot(iota(square, 1) < iota(square, 0)), picked_t)
    slots = jnp.where(picked, earlier, -1.0)
    slots_ref[...] = slots

    pl.semaphore_wait(barrier, 73)

    def token_copies(part, step):
        position = (here[part] + step) % 4
        to = device(*line_member(part, position, here, c))
        return [
            pltpu.make_async_remote_copy(
                src_ref=x_ref.at[:, pl.ds(first, COL)],
                dst_ref=gathered.at[part, here[part], pl.ds(128 * n, 128)],
                send_sem=ax_send.at[part, step, n],
                recv_sem=ax_recv.at[part, here[part], n],
                device_id=to,
                device_id_type=MESH,
            )
            for n, first in enumerate((part * COL, LAST))
        ]

    for step in (1, 3, 2):
        for part in range(3):
            for copy in token_copies(part, step):
                copy.start()

    logits = nn(h_ref[...], rw_ref[...])
    highest = jnp.max(jnp.where(picked, logits, -jnp.inf), axis=1, keepdims=True)
    raised = jnp.where(picked, jnp.exp(jnp.where(picked, logits, highest) - highest), 0.0)
    combine = raised / jnp.sum(raised, axis=1, keepdims=True)
    combine_ref[...] = combine
    for part in range(3):
        meta[part, here[part], 0:128, :] = slots.astype(BF16)
        meta[part, here[part], 128:256, :] = combine.astype(BF16)

    def meta_copy(part, step):
        position = (here[part] + step) % 4
        return pltpu.make_async_remote_copy(
            src_ref=meta.at[part, here[part]],
            dst_ref=meta.at[part, here[part]],
            send_sem=am_send.at[part, step],
            recv_sem=am_recv.at[part, here[part]],
            device_id=device(*line_member(part, position, here, c)),
            device_id_type=MESH,
        )

    for step in (1, 3, 2):
        for part in range(3):
            meta_copy(part, step).start()

    for part in range(3):
        gathered[part, here[part], 0:128, :] = x_ref[:, part * COL : (part + 1) * COL]
        gathered[part, here[part], 128:256, :] = x_ref[:, LAST:]

    row, lane = iota((512, 128), 0), iota((512, 128), 1)
    ahead = sign * (row // 128) + 4
    core = (c + (row // 64) % 2) % 2
    b = (row // 16) % 4
    for part in range(3):
        owner = expert_id(*plane_member(part, ahead, b, here, core))
        expand[part] = onehot(owner == lane).reshape(4, 2, 64, 128)

    def message(buffer, part, a, dc, b):
        if part == 1:
            return buffer.at[1, a, :, dc, :, b]
        return buffer.at[part, a, dc, b // 2, b % 2]

    def dispatch_place(part, k):
        mixed = (k % 16) * 7 % 16
        return mixed // 4, k // 16, (second[part] + sign * (mixed % 4) + 4) % 4

    def dispatch_copy(part, k):
        a, dc, b = dispatch_place(part, k)
        to = plane_member(part, sign * a + 4, b, here, (c + dc) % 2)
        landing = (
            landed.at[0, :, yh, c, yl, z],
            landed.at[1, x, :, c, :, z],
            landed.at[2, x, yh, c, yl],
        )[part]
        return pltpu.make_async_remote_copy(
            src_ref=message(staged, part, a, dc, b),
            dst_ref=landing,
            send_sem=d_send.at[part, k],
            recv_sem=d_recv.at[part, a * 8 + dc * 4 + second[part]],
            device_id=device(*to),
            device_id_type=MESH,
        )

    def own_copy(part):
        landing = (
            landed.at[0, :, yh, c, yl, z],
            landed.at[1, x, :, c, :, z],
            landed.at[2, x, yh, c, yl],
        )[part]
        return pltpu.make_async_copy(
            message(staged, part, 0, 0, second[part]), landing, own_sem.at[part]
        )

    slot_of_row = iota((256, 128), 0) % 16

    def wait_line(part):
        for step in (1, 2, 3):
            position = (here[part] + step) % 4
            for n in range(2):
                pltpu.make_async_remote_copy(
                    src_ref=gathered.at[part, position, pl.ds(128 * n, 128)],
                    dst_ref=gathered.at[part, position, pl.ds(128 * n, 128)],
                    send_sem=ax_send.at[part, step, n],
                    recv_sem=ax_recv.at[part, position, n],
                    device_id=device(*line_member(part, position, here, c)),
                    device_id_type=MESH,
                ).wait_recv()
            pltpu.make_async_remote_copy(
                src_ref=meta.at[part, position],
                dst_ref=meta.at[part, position],
                send_sem=am_send.at[part, step],
                recv_sem=am_recv.at[part, position],
                device_id=device(*line_member(part, position, here, c)),
                device_id_type=MESH,
            ).wait_recv()

    def extra_slot(part):
        return jnp.where(slot_of_row >= SLOTS, slot_of_row - SLOTS + 4 * part, -9).astype(F32)

    for part in range(3):
        wait_line(part)

    for dc in range(2):
        for part in range(3):

            def select(j, carry, part=part, dc=dc):
                spread = nt(expand[part, :, dc].reshape(256, 128), meta[part, j, 0:128, :])
                main = onehot(spread == slot_of_row.astype(F32))
                extra = onehot(spread == extra_slot(part))
                chosen = jnp.concatenate([main, extra], axis=1)
                made = nn(chosen, gathered[part, j]).astype(BF16)
                if part == 1:
                    staged[1, :, j // 2, dc, j % 2] = made.reshape(4, 4, 16, COL)
                else:
                    staged[part, :, dc, :, :, j] = made.reshape(4, 2, 2, 16, COL)
                return carry

            lax.fori_loop(0, 4, select, 0)

        def send(k, carry):
            for part in range(3):
                dispatch_copy(part, k).start()
            return carry

        lax.fori_loop(1 if dc == 0 else 16, 16 if dc == 0 else 32, send, 0)
        if dc == 0:
            for part in range(3):
                own_copy(part).start()

    def saved_copies(g, buffer):
        rows = pl.ds(pl.multiple_of(g % 4 * 32, 32), 32)
        return (
            pltpu.make_async_copy(gs_hbm.at[:, rows, :], gs_buf.at[buffer], gs_sem.at[0, buffer]),
            pltpu.make_async_copy(us_hbm.at[:, rows, :], us_buf.at[buffer], gs_sem.at[1, buffer]),
        )

    for copy in saved_copies(0, 0):
        copy.start()
    for copy in weight_copies():
        copy.wait()
    for part in range(3):
        own_copy(part).wait()

    def settle_dispatch(k, carry):
        for part in range(3):
            a, dc, b = dispatch_place(part, k)
            pltpu.make_async_remote_copy(
                src_ref=message(staged, part, a, dc, b),
                dst_ref=message(landed, part, a, dc, b),
                send_sem=d_send.at[part, k],
                recv_sem=d_recv.at[part, a * 8 + dc * 4 + b],
                device_id=device(x, y, z, 1 - c),
                device_id_type=MESH,
            ).wait_recv()
        return carry

    def settle_send(k, carry):
        for part in range(3):
            dispatch_copy(part, k).wait_send()
        return carry

    big = (256, 256)
    to_row, from_row = iota(big, 0), iota(big, 1)
    same_source = to_row // 16 == from_row // 16
    moves = [
        onehot(
            same_source
            & (from_row % 16 >= SLOTS)
            & (to_row % 16 == from_row % 16 - SLOTS + 4 * part)
        )
        for part in range(3)
    ]
    take = (256, 32 * SLOTS)
    take_row, take_from = iota(take, 0), iota(take, 1)
    source_row = take_row // 128 * 16 + take_row // 16 % 8
    same_slot = take_row % 16 == take_from // 32
    diagonal = iota((128, 128), 0) == iota((128, 128), 1)

    def expert_group(g, carry):
        gx = g % 4
        core = jnp.where(g < 4, c, 1 - c)
        buffer = g % 2

        @pl.when(g < 7)
        def _():
            for copy in saved_copies(g + 1, (g + 1) % 2):
                copy.start()

        for copy in saved_copies(g, buffer):
            copy.wait()
        rows = [landed[part, gx, :, core].reshape(256, COL) for part in range(3)]
        last = (nn(moves[0], rows[0]) + nn(moves[1], rows[1]) + nn(moves[2], rows[2])).astype(BF16)
        projected = (
            nt(rows[0], wd[0]) + nt(rows[1], wd[1]) + nt(rows[2], wd[2]) + nt(last, wd[3])
        )
        by_source = onehot(same_slot & (take_from % 32 == source_row + 8 * core))
        gate = nn(by_source, gs_buf[buffer].reshape(32 * SLOTS, HID))
        up = nn(by_source, us_buf[buffer].reshape(32 * SLOTS, HID))
        sigmoid = jax.nn.sigmoid(gate)
        activated = gate * sigmoid
        up_grad = projected * activated
        inner = jnp.sum(up_grad * up, axis=1, keepdims=True)
        gate_grad = projected * up * sigmoid * (1.0 + gate * (1.0 - sigmoid))
        shape = (2, 2, 4, 16, HID)
        landed[0, gx, :, core, :, :, :, 0:HID] = gate_grad.astype(BF16).reshape(shape)
        landed[1, gx, :, core, :, :, :, 0:HID] = up_grad.astype(BF16).reshape(shape)
        for n in range(2):
            column = inner[128 * n : 128 * n + 128]
            line = jnp.sum(jnp.where(diagonal, column, 0.0), axis=0, keepdims=True)
            score_rows[pl.ds(gx * 4 + n * 2 + core, 1), :] = line
        return carry

    lax.fori_loop(1, 16, settle_dispatch, 0)
    lax.fori_loop(0, 4, expert_group, 0)
    lax.fori_loop(16, 32, settle_dispatch, 0)
    lax.fori_loop(4, 8, expert_group, 0)

    score_send[...] = score_rows[...].astype(BF16)

    def plane_peer(k):
        to = plane_member(0, k // 8, (z + k % 4) % 4, here, (c + (k // 4) % 2) % 2)
        ids = device(*to)
        return ids, (ids[0] % 4) * 8 + ids[1]

    def score_copy(k):
        ids, _ = plane_peer(k)
        return pltpu.make_async_remote_copy(
            src_ref=score_send,
            dst_ref=score_plane.at[my_plane],
            send_sem=sp_send.at[k],
            recv_sem=sp_recv.at[my_plane],
            device_id=ids,
            device_id_type=MESH,
        )

    def start_score(k, carry):
        score_copy(k).start()
        return carry

    lax.fori_loop(1, 32, start_score, 0)
    score_plane[my_plane] = score_send[...]

    def return_place(part, k):
        a, dc = k // 8, (k // 4) % 2
        relay_core = (c + dc) % 2
        turn = 1 - 2 * relay_core
        return a, dc, (second[part] + turn * (k % 4) + 4) % 4, relay_core, 4 - turn * a

    def return_copy(part, k):
        a, dc, b, relay_core, ahead = return_place(part, k)
        return pltpu.make_async_remote_copy(
            src_ref=message(staged, part, a, dc, b),
            dst_ref=message(back_hbm, part, a, dc, second[part]),
            send_sem=r_send.at[part, k],
            recv_sem=r_recv.at[part, a * 8 + dc * 4 + second[part]],
            device_id=device(*plane_member(part, ahead, b, here, relay_core)),
            device_id_type=MESH,
        )

    def own_return(part):
        b = second[part]
        return pltpu.make_async_copy(
            message(staged, part, 0, 0, b), message(back_hbm, part, 0, 0, b), own_sem.at[part]
        )

    row_slot = iota((256, COL), 0) % 16

    def expert_unit(u, carry):
        a, dc = u // 2, u % 2
        relay_core = (c + dc) % 2
        ahead = 4 - (1 - 2 * relay_core) * a
        for part in range(3):
            if part == 0:
                ry = (y + ahead) % 4
                pair = [landed[n, :, ry // 2, relay_core, ry % 2, :, :, 0:HID] for n in range(2)]
            elif part == 1:
                rz = (z + ahead) % 4
                pair = [landed[n, :, :, relay_core, :, rz, :, 0:HID] for n in range(2)]
            else:
                rx = (x + ahead) % 4
                pair = [landed[n, rx, :, relay_core, :, :, :, 0:HID] for n in range(2)]
            gate_grad, up_grad = (v.reshape(256, HID) for v in pair)
            main = nt(gate_grad, wg[part * COL : (part + 1) * COL, :]) + nt(
                up_grad, wu[part * COL : (part + 1) * COL, :]
            )
            last = nt(gate_grad, wg[LAST:, :]) + nt(up_grad, wu[LAST:, :])
            made = jnp.where(
                row_slot < SLOTS, main, pltpu.roll(last, SLOTS - 4 * part, axis=0)
            ).astype(BF16)
            if part == 0:
                made = made.reshape(4, 4, 16, COL)
                for b in range(4):
                    staged[0, a, dc, b // 2, b % 2] = made[:, b]
            elif part == 1:
                made = made.reshape(4, 2, 2, 16, COL)
                for b in range(4):
                    staged[1, a, :, dc, :, b] = made[b]
            else:
                staged[2, a, dc] = made.reshape(2, 2, 4, 16, COL)

            @pl.when(u == 0)
            def _(part=part):
                own_return(part).start()

            def send(k, carry, part=part):
                return_copy(part, k).start()
                return carry

            lax.fori_loop(jnp.where(u == 0, 1, 4 * u), 4 * u + 4, send, 0)
        return carry

    lax.fori_loop(1, 32, settle_send, 0)
    lax.fori_loop(0, 4, expert_unit, 0)

    def settle_score(k, carry):
        score_copy(k).wait_send()
        ids, index = plane_peer(k)
        pltpu.make_async_remote_copy(
            src_ref=score_send,
            dst_ref=score_plane.at[index],
            send_sem=sp_send.at[k],
            recv_sem=sp_recv.at[index],
            device_id=ids,
            device_id_type=MESH,
        ).wait_recv()
        return carry

    lax.fori_loop(1, 32, settle_score, 0)
    plane_scores = score_plane[...].reshape(512, 128)
    for position in range(4):
        wanted = position * 4 + yh * 2 + c
        pickup = onehot(iota((32, 512), 1) == iota((32, 512), 0) * 16 + wanted)
        score_line[position] = nn(pickup, plane_scores).astype(BF16)

    def line_ids(step):
        return device((x + step) % 4, y, z, c)

    def line_score_copy(step):
        return pltpu.make_async_remote_copy(
            src_ref=score_line.at[(x + step) % 4],
            dst_ref=score_all.at[x],
            send_sem=sl_send.at[step],
            recv_sem=sl_recv.at[x],
            device_id=line_ids(step),
            device_id_type=MESH,
        )

    for step in (1, 2, 3):
        line_score_copy(step).start()
    score_all[x] = score_line[x]

    lax.fori_loop(4, 6, expert_unit, 0)

    for step in (1, 2, 3):
        position = (x + step) % 4
        line_score_copy(step).wait_send()
        pltpu.make_async_remote_copy(
            src_ref=score_line.at[position],
            dst_ref=score_all.at[position],
            send_sem=sl_send.at[step],
            recv_sem=sl_recv.at[position],
            device_id=line_ids(step),
            device_id_type=MESH,
        ).wait_recv()

    mine = onehot(iota((16, 128), 1) == iota((16, 128), 0) + seq * 16)
    by_slot = nt(mine, score_all[...].reshape(128, 128))
    slots = slots_ref[...]
    combine = combine_ref[...]
    score = jnp.zeros(square, F32)
    for n in range(SLOTS):
        score = score + jnp.where(slots == float(n), by_slot[n : n + 1, :], 0.0)
    weighted = combine * score
    logit_grad = (weighted - combine * jnp.sum(weighted, axis=1, keepdims=True)).astype(BF16)
    logit_grad_t = nt(onehot(iota(square, 0) == iota(square, 1)), logit_grad).astype(BF16)
    for n in range(4):
        terms = nn(logit_grad_t, h_ref[:, n * COL : (n + 1) * COL]).astype(BF16)
        for m in range(8):
            landed[2, m // 2, n // 2, n % 2, m % 2, 0] = terms[16 * m : 16 * m + 16]

    def terms_copy(step):
        return pltpu.make_async_remote_copy(
            src_ref=landed.at[2, (x + step) % 4, :, :, :, 0],
            dst_ref=terms_in.at[x],
            send_sem=t_send.at[step],
            recv_sem=t_recv.at[x],
            device_id=line_ids(step),
            device_id_type=MESH,
        )

    for step in (1, 2, 3):
        terms_copy(step).start()
    lax.fori_loop(6, 8, expert_unit, 0)
    total = landed[2, x, :, :, :, 0].astype(F32)
    for step in (1, 2, 3):
        position = (x + step) % 4
        terms_copy(step).wait_send()
        pltpu.make_async_remote_copy(
            src_ref=landed.at[2, position, :, :, :, 0],
            dst_ref=terms_in.at[position],
            send_sem=t_send.at[step],
            recv_sem=t_recv.at[position],
            device_id=line_ids(step),
            device_id_type=MESH,
        ).wait_recv()
        total = total + terms_in[position].astype(F32)
    for n in range(8):
        for m in range(2):
            block = total[n // 4, (n // 2) % 2, m]
            rows_out[16 * m : 16 * m + 16, n, :] = block[:, 512 * (n % 2) : 512 * (n % 2) + 512]

    def rows_copy(k):
        ids, index = plane_peer(k)
        return pltpu.make_async_remote_copy(
            src_ref=rows_out.at[index],
            dst_ref=rows_in.at[my_plane],
            send_sem=q_send.at[k],
            recv_sem=q_recv.at[my_plane],
            device_id=ids,
            device_id_type=MESH,
        )

    def start_rows(k, carry):
        rows_copy(k).start()
        return carry

    lax.fori_loop(1, 32, start_rows, 0)
    rows_in[my_plane] = rows_out[my_plane]

    lane_slot = iota((128, 512), 1) % 16
    for part in range(3):
        lane_extra = jnp.where(lane_slot >= SLOTS, lane_slot - SLOTS + 4 * part, -9)

        def weigh(j, carry, part=part, lane_extra=lane_extra):
            rows_of = expand[part].reshape(512, 128)
            spread = nt(meta[part, j, 0:128, :], rows_of)
            weight = nt(meta[part, j, 128:256, :], rows_of)
            main = jnp.where(spread == lane_slot.astype(F32), weight, 0.0).astype(BF16)
            extra = jnp.where(spread == lane_extra.astype(F32), weight, 0.0).astype(BF16)
            gathered[part, j, 0:128, 0:512] = main
            gathered[part, j, 128:256, 0:512] = extra
            return carry

        lax.fori_loop(0, 4, weigh, 0)

    for part in range(3):
        own_return(part).wait()

    def settle_return(k, carry):
        for part in range(3):
            a, dc, b, _, _ = return_place(part, k)
            pltpu.make_async_remote_copy(
                src_ref=message(staged, part, a, dc, b),
                dst_ref=message(back_hbm, part, a, dc, b),
                send_sem=r_send.at[part, k],
                recv_sem=r_recv.at[part, a * 8 + dc * 4 + b],
                device_id=device(x, y, z, 1 - c),
                device_id_type=MESH,
            ).wait_recv()
        return carry

    def load_copy(part, a):
        return pltpu.make_async_copy(
            back_hbm.at[part, a], landed.at[part, a], load_sem.at[part, a]
        )

    for a in range(4):
        lax.fori_loop(max(1, 8 * a), 8 * a + 8, settle_return, 0)
        for part in range(3):
            load_copy(part, a).start()

    def line_slot(part, position):
        n = part * 4 + position
        return wd.at[n // 3, pl.ds(pl.multiple_of((n % 3) * 256, 256), 256)]

    def part_copy(part, step):
        position = (here[part] + step) % 4
        return pltpu.make_async_remote_copy(
            src_ref=gathered.at[part, position],
            dst_ref=line_slot(part, here[part]),
            send_sem=p_send.at[part, step],
            recv_sem=p_recv.at[part, here[part]],
            device_id=device(*line_member(part, position, here, c)),
            device_id_type=MESH,
        )

    def gather_back(part, step):
        j = (here[part] + step) % 4
        if part == 1:
            rows = landed[1, :, j // 2, :, j % 2]
        else:
            rows = landed[part, :, :, :, :, j]
        weights = gathered[part, j, :, 0:512]
        gathered[part, j] = nn(weights, rows.reshape(512, COL)).astype(BF16)

    for part in range(3):
        for a in range(4):
            load_copy(part, a).wait()
    for step in (2, 1, 3):
        for part in range(3):
            gather_back(part, step)
            part_copy(part, step).start()
    for part in range(3):
        gather_back(part, 0)

    def settle_return_send(k, carry):
        for part in range(3):
            return_copy(part, k).wait_send()
        return carry

    lax.fori_loop(1, 32, settle_return_send, 0)

    routed = [nt(logit_grad, rw_ref[n * COL : (n + 1) * COL, :]) for n in range(4)]
    tail = routed[3]
    for part in range(3):
        head = routed[part] + gathered[part, here[part], 0:128, :].astype(F32)
        tail = tail + gathered[part, here[part], 128:256, :].astype(F32)
        for step in (1, 2, 3):
            position = (here[part] + step) % 4
            part_copy(part, step).wait_send()
            arrived = line_slot(part, position)
            pltpu.make_async_remote_copy(
                src_ref=gathered.at[part, position],
                dst_ref=arrived,
                send_sem=p_send.at[part, step],
                recv_sem=p_recv.at[part, position],
                device_id=device(*line_member(part, position, here, c)),
                device_id_type=MESH,
            ).wait_recv()
            head = head + arrived[0:128, :].astype(F32)
            tail = tail + arrived[128:256, :].astype(F32)
        out_ref[:, part * COL : (part + 1) * COL] = head.astype(BF16)
    out_ref[:, LAST:] = tail.astype(BF16)

    def settle_rows(k, carry):
        rows_copy(k).wait_send()
        ids, index = plane_peer(k)
        pltpu.make_async_remote_copy(
            src_ref=rows_out.at[index],
            dst_ref=rows_in.at[index],
            send_sem=q_send.at[k],
            recv_sem=q_recv.at[index],
            device_id=ids,
            device_id_type=MESH,
        ).wait_recv()
        return carry

    lax.fori_loop(1, 32, settle_rows, 0)
    router_ref[...] = jnp.sum(rows_in[...], axis=0)

    for part in range(3):
        for step in (1, 2, 3):
            for copy in token_copies(part, step):
                copy.wait_send()
            meta_copy(part, step).wait_send()


def shards(
    grad_out,
    moe_input,
    router_weight,
    routes,
    gate_saved,
    up_saved,
    expert_gate,
    expert_up,
    expert_down,
):
    dma = pltpu.SemaphoreType.DMA
    whole = pl.BlockSpec(memory_space=pltpu.VMEM)
    away = pl.BlockSpec(memory_space=pl.ANY)
    blocks = (3, 4, 2, 2, 2, 4, 16, COL)
    input_grad, router_grad, _ = pl.pallas_call(
        kernel,
        out_shape=(
            jax.ShapeDtypeStruct((128, 4096), BF16),
            jax.ShapeDtypeStruct((8, 512), F32),
            jax.ShapeDtypeStruct(blocks, BF16),
        ),
        in_specs=[whole] * 4 + [away] * 5,
        out_specs=(whole, whole, away),
        scratch_shapes=[
            pltpu.VMEM((3, 4, 256, COL), BF16),
            pltpu.VMEM((3, 4, 256, 128), BF16),
            pltpu.VMEM(blocks, BF16),
            pltpu.VMEM(blocks, BF16),
            pltpu.VMEM((4, HID, COL), BF16),
            pltpu.VMEM((4096, HID), BF16),
            pltpu.VMEM((4096, HID), BF16),
            pltpu.VMEM((2, SLOTS, 32, HID), BF16),
            pltpu.VMEM((2, SLOTS, 32, HID), BF16),
            pltpu.VMEM((3, 4, 2, 64, 128), BF16),
            pltpu.VMEM((128, 128), F32),
            pltpu.VMEM((128, 128), F32),
            pltpu.VMEM((16, 128), F32),
            pltpu.VMEM((16, 128), BF16),
            pltpu.VMEM((32, 16, 128), BF16),
            pltpu.VMEM((4, 32, 128), BF16),
            pltpu.VMEM((4, 32, 128), BF16),
            pltpu.VMEM((4, 2, 2, 2, 16, COL), BF16),
            pltpu.VMEM((32, 8, 512), F32),
            pltpu.VMEM((32, 8, 512), F32),
            dma((6,)),
            dma((2, 2)),
            dma((3, 4, 2)),
            dma((3, 4, 2)),
            dma((3, 4)),
            dma((3, 4)),
            dma((3,)),
            dma((3, 32)),
            dma((3, 32)),
            dma((3, 32)),
            dma((3, 32)),
            dma((32,)),
            dma((32,)),
            dma((4,)),
            dma((4,)),
            dma((4,)),
            dma((4,)),
            dma((32,)),
            dma((32,)),
            dma((3, 4)),
            dma((3, 4)),
            dma((3, 4)),
        ],
        compiler_params=pltpu.CompilerParams(
            collective_id=0, has_side_effects=True, vmem_limit_bytes=63 << 20
        ),
        cost_estimate=pl.CostEstimate(
            flops=80_000_000_000, bytes_accessed=60 << 20, transcendentals=2 << 20
        ),
    )(
        grad_out,
        moe_input,
        router_weight,
        routes.T,
        jnp.transpose(gate_saved[0], (1, 0, 2)),
        jnp.transpose(up_saved[0], (1, 0, 2)),
        expert_gate[0],
        expert_up[0],
        expert_down[0],
    )
    return (input_grad, router_grad.reshape(1, 4096))


def solution(mesh):
    placed = (
        P(("dp", "seq"), None),
        P(("dp", "seq"), None),
        P(),
        P(("dp", "seq"), None),
        P(("dp", "seq"), None, None, None),
        P(("dp", "seq"), None, None, None),
        P(("dp", "seq"), None, None),
        P(("dp", "seq"), None, None),
        P(("dp", "seq"), None, None),
    )
    return jax.shard_map(
        shards,
        mesh=mesh,
        in_specs=placed,
        out_specs=(P(("dp", "seq"), None), P(("dp", "seq"), None)),
        check_vma=False,
    )
```
